256 devices in a mesh: dp: 16 (over y_lo, x, core), seq: 16 (over z, y_hi).
Axes of the slice: x: 4, y: 4 (y_hi: 2, y_lo: 2; y = y_hi * 2 + y_lo), z: 8, core: 2. Of those that a mesh axis runs over, the one named last changes fastest.
Arguments:
- primal: bfloat16 [16, 2048, 3, 4096], P('dp', 'seq'), as said below
- tangent: bfloat16 [16, 2048, 3, 4096], P('dp', 'seq'), may hold values from -6 to 6
- cotangent: bfloat16 [16, 2048, 2560], P('dp', 'seq'), may hold values from -6 to 6
Outputs:
- attended: bfloat16 [16, 2048, 4096], P('dp', 'seq')
- attended_tangent: bfloat16 [16, 2048, 4096], P('dp', 'seq')
- weight_grad: float32 [2560, 4096], P('dp', 'seq')
The draws below stay inside these ranges and needn't reach their ends.
Inputs may be any that keep to these rules, and one draw needn't show every extreme that they name: `primal`: slots 0, 1, 2 of the third dimension are queries, keys and values.
All inputs are finite; a program needn't handle non-finite values.
Results may differ from the reference program's by a relative error of at most 0.005.
Values may be sent and summed in bfloat16 or wider, within the bound.
A program may use at most 128 MiB of HBM per device.

```python
import jax
import jax.numpy as jnp
from jax import lax

HEADS = 32
HEAD_DIM = 128
FEAT_OUT = 2560
HIDDEN_WIDTH = 4096
SEQ_LEN = 2048
CLIPS = 16


def draw_primal(key, part):
    key = jax.random.fold_in(key, 11)
    key_base = jax.random.fold_in(key, 0)
    shape = (CLIPS, SEQ_LEN, 3, HIDDEN_WIDTH)
    return jax.random.normal(key_base, shape, jnp.float32).astype(jnp.bfloat16)


def raised(result, own_key, source, target, blocks, factor):
    owner, partner = [(jnp.arange(result.shape[position]) // (result.shape[position] // blocks)).reshape([-1 if axis == position else 1 for axis in range(result.ndim)]) for position in (source, target)]
    chosen = jax.random.permutation(own_key, blocks)[partner]
    strong = (owner == chosen) | (owner == (partner + blocks // 2) % blocks)
    return jnp.where(strong, factor * result, result)


def levels(own_key, shape, shards, least, top_value):
    def one(axis_at, shards_of):
        heights = jax.random.uniform(jax.random.fold_in(jax.random.fold_in(own_key, 6), axis_at), (shards_of,), jnp.float32, least / len(shards), top_value / len(shards))
        return jnp.repeat(jnp.exp(heights), shape[axis_at] // shards_of).reshape((-1,) + (1,) * (len(shape) - axis_at - 1))

    gain = one(*shards[0])
    for cut in shards[1:]:
        gain = gain * one(*cut)
    return gain


def centred(own_key, extent, deviation, bound, pieces=(), held_as=jnp.bfloat16):
    factor_of = levels(own_key, extent, pieces, -0.22, 0.18) if pieces else 1.0
    values = jax.random.normal(own_key, extent, jnp.float32) * deviation * factor_of
    return jnp.minimum(jnp.maximum(values, -bound), bound).astype(held_as)


def gaussian_with(stream_key, extent, deviation, bound, cuts, heavy, kind=jnp.bfloat16):
    values = deviation * jax.random.normal(stream_key, extent, jnp.float32)
    if cuts:
        values = values * levels(stream_key, extent, cuts, -0.22, 0.18)
    return jnp.clip(raised(values, jax.random.fold_in(stream_key, 3), *heavy), -bound, bound).astype(kind)


def setup_inputs(seed: int = 0) -> dict:
    streams_of = jax.random.split(jax.random.key(seed), 4)
    primal = draw_primal(jax.random.fold_in(streams_of[3], 71), 0)
    tangent = centred(streams_of[1], (CLIPS, SEQ_LEN, 3, HIDDEN_WIDTH), 1.0, 6.0, ((0, 16), (1, 16)))
    cotangent = gaussian_with(streams_of[2], (CLIPS, SEQ_LEN, FEAT_OUT), 1.0, 6.0, ((0, 16), (1, 16)), (0, 2, 16, 2.0))
    return dict(primal=primal, tangent=tangent, cotangent=cotangent)


def head_jvp(q, k, v, dq, dk, dv):
    scale = 1.0 / (HEAD_DIM ** 0.5)
    block = min(512, SEQ_LEN)
    qs = q.reshape(SEQ_LEN // block, block, HEAD_DIM)
    dqs = dq.reshape(SEQ_LEN // block, block, HEAD_DIM)

    def one_block(pair):
        qb, dqb = pair
        scores = jnp.dot(qb, k.T, precision=lax.Precision.HIGHEST) * scale
        probs = jax.nn.softmax(scores, axis=-1)
        probs_low = lax.optimization_barrier(probs.astype(jnp.bfloat16)).astype(jnp.float32)
        out = jnp.dot(probs_low, v, precision=lax.Precision.HIGHEST)
        dscores = (jnp.dot(dqb, k.T, precision=lax.Precision.HIGHEST) + jnp.dot(qb, dk.T, precision=lax.Precision.HIGHEST)) * scale
        centre = jnp.sum(probs * dscores, axis=-1, keepdims=True)
        dprobs = lax.optimization_barrier((probs * (dscores - centre)).astype(jnp.bfloat16)).astype(jnp.float32)
        dout = jnp.dot(probs_low, dv, precision=lax.Precision.HIGHEST) + jnp.dot(dprobs, v, precision=lax.Precision.HIGHEST)
        return out.astype(jnp.bfloat16), dout.astype(jnp.bfloat16)

    outs, douts = lax.map(one_block, (qs, dqs))
    return outs.reshape(SEQ_LEN, HEAD_DIM), douts.reshape(SEQ_LEN, HEAD_DIM)


def clip_jvp(pair):
    prim, tang = pair
    prim = prim.astype(jnp.float32).reshape(SEQ_LEN, 3, HEADS, HEAD_DIM).transpose(2, 1, 0, 3)
    tang = tang.astype(jnp.float32).reshape(SEQ_LEN, 3, HEADS, HEAD_DIM).transpose(2, 1, 0, 3)

    def one_head(items):
        pr, tg = items
        return head_jvp(pr[0], pr[1], pr[2], tg[0], tg[1], tg[2])

    outs, douts = lax.map(one_head, (prim, tang))
    return outs.transpose(1, 0, 2).reshape(SEQ_LEN, HIDDEN_WIDTH), douts.transpose(1, 0, 2).reshape(SEQ_LEN, HIDDEN_WIDTH)


def reference(primal, tangent, cotangent):
    attended, attended_tangent = lax.map(clip_jvp, (primal, tangent))
    flat_cot = cotangent.reshape(CLIPS * SEQ_LEN, FEAT_OUT)
    flat_out = attended.reshape(CLIPS * SEQ_LEN, HIDDEN_WIDTH)
    weight_grad = jnp.dot(flat_cot.T, flat_out, preferred_element_type=jnp.float32)
    return attended, attended_tangent, weight_grad
```

```python
import jax
import jax.numpy as jnp
from jax import lax
from jax.experimental import pallas as pl
from jax.experimental.pallas import tpu as pltpu
from jax.sharding import PartitionSpec as P

MESH = pl.DeviceIdType.MESH
HEAD_DIM = 128
TOKENS = 128
SEQ_LEN = 2048
WIDTH = 4096
FEATURES = 2560
HALF = FEATURES // 2
ROWS = 160
NSEQ = 16
NDP = 16
NZ = 8
LOCAL_HEADS = 2
BLOCK = 256
BLOCKS = SEQ_LEN // BLOCK
SCALE = 1.0 / HEAD_DIM**0.5


def wait_bytes(ref, sem):
    pltpu.make_async_copy(ref, ref, sem).wait()


def kernel(
    prim, tang, cot, att_out, tan_out, wg_out,
    qkv, cots, own, own_t, part, term, terms,
    qkv_send, qkv_recv, cot_send, cot_recv, cot_local,
    out_send, att_recv, tan_recv, part_send, part_recv, term_send, term_recv,
):
    dp, seq = lax.axis_index("dp"), lax.axis_index("seq")
    z, yh = seq // 2, seq % 2
    yl = dp // 8
    partner = seq + 1 - 2 * yh
    up, down = lax.rem(z + 1, NZ) * 2 + yh, lax.rem(z + NZ - 1, NZ) * 2 + yh
    mine = yl == yh

    barrier = pltpu.get_barrier_semaphore()

    def greet_seq(o, c):
        pl.semaphore_signal(
            barrier, inc=1, device_id=(dp, lax.rem(seq + o, NSEQ)), device_id_type=MESH
        )
        return c

    lax.fori_loop(1, NSEQ, greet_seq, 0)

    def greet_dp(i, c):
        @pl.when(jnp.logical_or(i != dp, jnp.logical_not(mine)))
        def _():
            pl.semaphore_signal(
                barrier, inc=1, device_id=(i, z * 2 + yl), device_id_type=MESH
            )

        return c

    lax.fori_loop(0, NDP, greet_dp, 0)

    @pl.when(mine)
    def _():
        pl.semaphore_wait(barrier, NSEQ - 1 + NDP - 1)

    @pl.when(jnp.logical_not(mine))
    def _():
        pl.semaphore_wait(barrier, NSEQ - 1 + NDP)

    def rows_of(device):
        return pl.ds(pl.multiple_of(device * TOKENS, TOKENS), TOKENS)

    def send_qkv(h):
        for a, array in enumerate((prim, tang)):
            pltpu.make_async_copy(
                array.at[:, :, pl.ds(pl.multiple_of(seq * 256 + h * 128, 128), 128)],
                qkv.at[h, :, rows_of(seq), pl.ds(a * 128, 128)],
                qkv_recv.at[h],
            ).start()

        def one(o, c):
            to = lax.rem(seq + o, NSEQ)
            for a, array in enumerate((prim, tang)):
                pltpu.make_async_remote_copy(
                    array.at[:, :, pl.ds(pl.multiple_of(to * 256 + h * 128, 128), 128)],
                    qkv.at[h, :, rows_of(seq), pl.ds(a * 128, 128)],
                    qkv_send.at[h],
                    qkv_recv.at[h],
                    device_id=(dp, to),
                    device_id_type=MESH,
                ).start()
            return c

        lax.fori_loop(1, NSEQ, one, 0)

    def half(which):
        return pl.ds(pl.multiple_of(which * HALF, HALF), HALF)

    send_qkv(0)
    to_partner = pltpu.make_async_remote_copy(
        cot.at[:, half(1 - yh)], cots.at[rows_of(seq)], cot_send.at[14], cot_recv.at[14],
        device_id=(dp, partner), device_id_type=MESH,
    )
    to_partner.start()
    local = pltpu.make_async_copy(cot.at[:, half(yh)], cots.at[rows_of(seq)], cot_local)
    local.start()

    def ring_copy(ring, way, step):
        source = lax.rem(z + (step if way else NZ - step), NZ) * 2
        source = source + (1 - yh if ring else yh)
        index = ring * 7 + (step + steps[ring, 0] if way else step)
        return pltpu.make_async_remote_copy(
            cots.at[rows_of(source)], cots.at[rows_of(source)],
            cot_send.at[index], cot_recv.at[index],
            device_id=(dp, down if way else up), device_id_type=MESH,
        )

    steps = {(0, 0): 4, (0, 1): 3, (1, 0): 3, (1, 1): 4}
    local.wait()
    copies = []
    for step in range(4):
        for ring in (0, 1):
            if step == 0 and ring == 1:
                send_qkv(1)
                to_partner.wait()
            for way in (0, 1):
                if step < steps[ring, way]:
                    if step:
                        ring_copy(ring, way, step - 1).wait_recv()
                    copy = ring_copy(ring, way, step)
                    copy.start()
                    copies.append((copy, step == steps[ring, way] - 1))
    for copy, last in copies:
        copy.wait_send()
        if last:
            copy.wait_recv()

    def attend(h):
        def one(step, carry):
            even = lax.rem(step, 2) == 0
            b = lax.rem(z + jnp.where(even, 4 - step // 2, 5 + step // 2), NZ)
            rows = pl.ds(pl.multiple_of(b * BLOCK, BLOCK), BLOCK)
            q = qkv[h, 0, rows, :]
            query, dquery = q[:, :HEAD_DIM], q[:, HEAD_DIM:]
            contract = (((1,), (1,)), ((), ()))
            scores = lax.dot_general(
                query, qkv[h, 1, :, :HEAD_DIM], contract, preferred_element_type=jnp.float32
            )
            dscores = lax.dot_general(
                jnp.concatenate([dquery, query], axis=1), qkv[h, 1], contract,
                preferred_element_type=jnp.float32,
            ) * SCALE
            top = jnp.max(scores, axis=-1, keepdims=True)
            expo = jnp.exp((scores - top) * SCALE)
            probs = expo * (1.0 / jnp.sum(expo, axis=-1, keepdims=True))
            centre = jnp.sum(probs * dscores, axis=-1, keepdims=True)
            dprobs = (probs * (dscores - centre)).astype(jnp.bfloat16)
            both = jnp.dot(
                probs.astype(jnp.bfloat16), qkv[h, 2], preferred_element_type=jnp.float32
            )
            dout = both[:, HEAD_DIM:] + jnp.dot(
                dprobs, qkv[h, 2, :, :HEAD_DIM], preferred_element_type=jnp.float32
            )
            own[h, rows, :] = both[:, :HEAD_DIM].astype(jnp.bfloat16)
            own_t[h, rows, :] = dout.astype(jnp.bfloat16)

            columns = pl.ds(pl.multiple_of(seq * 256 + h * 128, 128), 128)
            for y in (0, 1):
                to = b * 2 + y

                @pl.when(to != seq)
                def _():
                    for source, target, recv in (
                        (own, att_out, att_recv), (own_t, tan_out, tan_recv)
                    ):
                        pltpu.make_async_remote_copy(
                            source.at[h, rows_of(to)], target.at[:, columns],
                            out_send, recv, device_id=(dp, to), device_id_type=MESH,
                        ).start()

                @pl.when(to == seq)
                def _():
                    for source, target, recv in (
                        (own, att_out, att_recv), (own_t, tan_out, tan_recv)
                    ):
                        pltpu.make_async_copy(
                            source.at[h, rows_of(to)], target.at[:, columns], recv
                        ).start()

            pltpu.make_async_remote_copy(
                own.at[h, rows], part.at[h, rows], part_send.at[h], part_recv.at[h],
                device_id=(dp, partner), device_id_type=MESH,
            ).start()
            return carry

        lax.fori_loop(0, BLOCKS, one, 0)

    def weigh(h):
        wait_bytes(part.at[h], part_recv.at[h])
        both = jnp.concatenate([own[h], part[h]], axis=1)

        def one(n, carry):
            span = pl.ds(pl.multiple_of(n * 256, 256), 256)
            term[h, span, :] = lax.dot_general(
                cots[:, span], both, (((0,), (0,)), ((), ())),
                preferred_element_type=jnp.float32,
            )
            return carry

        lax.fori_loop(0, HALF // 256, one, 0)

        def send(n, carry):
            block = pl.ds(pl.multiple_of(n * ROWS, ROWS), ROWS)
            to = yh * 8 + n
            is_mine = jnp.logical_and(mine, to == dp)

            @pl.when(is_mine)
            def _():
                pltpu.make_async_copy(
                    term.at[h, block, pl.ds(0, 128)], terms.at[h, dp], term_recv.at[h]
                ).start()

            @pl.when(jnp.logical_not(is_mine))
            def _():
                pltpu.make_async_remote_copy(
                    term.at[h, block, pl.ds(0, 128)], terms.at[h, dp],
                    term_send.at[h], term_recv.at[h],
                    device_id=(to, seq), device_id_type=MESH,
                ).start()

            pltpu.make_async_remote_copy(
                term.at[h, block, pl.ds(128, 128)], terms.at[h, dp],
                term_send.at[h], term_recv.at[h],
                device_id=(to, partner), device_id_type=MESH,
            ).start()
            return carry

        lax.fori_loop(0, 8, send, 0)

    for h in range(LOCAL_HEADS):
        wait_bytes(qkv.at[h], qkv_recv.at[h])
        attend(h)
        weigh(h)

    for h in range(LOCAL_HEADS):
        wait_bytes(terms.at[h], term_recv.at[h])
        total = terms[h, 0]
        for s in range(1, NDP):
            total = total + terms[h, s]
        wg_out[:, pl.ds(h * 128, 128)] = total

    wait_bytes(att_out, att_recv)
    wait_bytes(tan_out, tan_recv)
    sent = pl.ds(0, (NSEQ - 1) * TOKENS)
    for h in range(LOCAL_HEADS):
        wait_bytes(qkv.at[h, :, sent], qkv_send.at[h])
        wait_bytes(part.at[h], part_send.at[h])

        @pl.when(mine)
        def _():
            wait_bytes(terms.at[h, pl.ds(0, NDP - 1)], term_send.at[h])

        @pl.when(jnp.logical_not(mine))
        def _():
            wait_bytes(terms.at[h], term_send.at[h])

    wait_bytes(qkv.at[:, 0, sent], out_send)


def body(primal, tangent, cotangent):
    prim = jnp.transpose(primal[0], (1, 0, 2))
    tang = jnp.transpose(tangent[0], (1, 0, 2))
    hbm = pl.BlockSpec(memory_space=pl.ANY)
    dma = pltpu.SemaphoreType.DMA
    bf16, f32 = jnp.bfloat16, jnp.float32
    att, tan, wg = pl.pallas_call(
        kernel,
        out_shape=(
            jax.ShapeDtypeStruct((TOKENS, WIDTH), bf16),
            jax.ShapeDtypeStruct((TOKENS, WIDTH), bf16),
            jax.ShapeDtypeStruct((ROWS, 256), f32),
        ),
        in_specs=[hbm] * 3,
        out_specs=(hbm, hbm, pl.BlockSpec(memory_space=pltpu.VMEM)),
        scratch_shapes=[
            pltpu.VMEM((LOCAL_HEADS, 3, SEQ_LEN, 256), bf16),
            pltpu.VMEM((SEQ_LEN, HALF), bf16),
            pltpu.VMEM((LOCAL_HEADS, SEQ_LEN, HEAD_DIM), bf16),
            pltpu.VMEM((LOCAL_HEADS, SEQ_LEN, HEAD_DIM), bf16),
            pltpu.VMEM((LOCAL_HEADS, SEQ_LEN, HEAD_DIM), bf16),
            pltpu.VMEM((LOCAL_HEADS, HALF, 256), f32),
            pltpu.VMEM((LOCAL_HEADS, NDP, ROWS, HEAD_DIM), f32),
            dma((2,)), dma((2,)), dma((15,)), dma((15,)), dma(()),
            dma(()), dma(()), dma(()), dma((2,)), dma((2,)), dma((2,)), dma((2,)),
        ],
        compiler_params=pltpu.CompilerParams(
            collective_id=0, has_side_effects=True, vmem_limit_bytes=56 * 2**20
        ),
        cost_estimate=pl.CostEstimate(
            flops=2 * 2 * SEQ_LEN * SEQ_LEN * 128 * 6 + 2 * FEATURES * 256 * SEQ_LEN,
            bytes_accessed=16 * 2**20, transcendentals=2 * SEQ_LEN * SEQ_LEN,
        ),
        name="attention_jvp",
    )(prim, tang, cotangent[0])
    return att[None], tan[None], wg


def solution(mesh):
    return jax.shard_map(
        body,
        mesh=mesh,
        in_specs=(P("dp", "seq", None, None), P("dp", "seq", None, None), P("dp", "seq", None)),
        out_specs=(P("dp", "seq", None), P("dp", "seq", None), P("dp", "seq")),
        check_vma=False,
    )
```

```python
import jax
import jax.numpy as jnp
from jax import lax
from jax.experimental import pallas as pl
from jax.experimental.pallas import tpu as pltpu
from jax.sharding import PartitionSpec as P

MESH = pl.DeviceIdType.MESH
HEAD_DIM = 128
TOKENS = 128
SEQ_LEN = 2048
WIDTH = 4096
FEATURES = 2560
QUARTER = FEATURES // 4
ROWS = 160
NSEQ = 16
NDP = 16
PLANE = 32
PLANE_TOKENS = PLANE * TOKENS
NZ = 8
LOCAL_HEADS = 2
BLOCK = 256
BLOCKS = SEQ_LEN // BLOCK
SCALE = 1.0 / HEAD_DIM**0.5


def wait_bytes(ref, sem):
    pltpu.make_async_copy(ref, ref, sem).wait()


def kernel(
    prim, tang, cot, att_out, tan_out, wg_out,
    qkv, cots, own, own_t, atts, term, terms,
    qkv_send, qkv_recv, cot_send, cot_recv, out_send, att_recv, tan_recv,
    spread_send, spread_recv, core_send, core_recv, term_send, term_recv,
):
    dp, seq = lax.axis_index("dp"), lax.axis_index("seq")
    z, yh = seq // 2, seq % 2
    yl, x, c = dp // 8, (dp // 2) % 4, dp % 2
    here = dp * 2 + yh
    mine = jnp.logical_and(x == 0, c == 0)

    def columns_at(x_at, way):
        apart = jnp.where(x_at == 0, 4, NZ - x_at)
        return jnp.where(way == 0, x_at, apart)

    def summed_at(offset):
        near = jnp.where(offset > 4, NZ - offset, offset)
        return lax.rem(near, 4)

    def rows_of(device):
        return pl.ds(pl.multiple_of(device * TOKENS, TOKENS), TOKENS)

    def head_columns(device, h):
        return pl.ds(pl.multiple_of(device * 256 + h * 128, 128), 128)

    barrier = pltpu.get_barrier_semaphore()

    def greet(dp_to, seq_to):
        pl.semaphore_signal(barrier, inc=1, device_id=(dp_to, seq_to), device_id_type=MESH)

    def greet_clip(o, carry):
        greet(dp, lax.rem(seq + o, NSEQ))
        return carry

    def greet_plane(o, carry):
        there = lax.rem(here + o, PLANE)
        greet(there // 2, z * 2 + there % 2)
        return carry

    def greet_terms(o, carry):
        source_dp = (yl * 4 + summed_at(o)) * 2 + x // 2

        @pl.when(jnp.logical_not(jnp.logical_and(mine, o == 0)))
        def _():
            greet(source_dp, lax.rem(z + NZ - o, NZ) * 2 + yh)

        return carry

    lax.fori_loop(1, NSEQ, greet_clip, 0)
    lax.fori_loop(1, PLANE, greet_plane, 0)
    lax.fori_loop(0, NZ, greet_terms, 0)

    @pl.when(mine)
    def _():
        pl.semaphore_wait(barrier, NSEQ - 1 + PLANE - 1 + NZ - 1)

    @pl.when(jnp.logical_not(mine))
    def _():
        pl.semaphore_wait(barrier, NSEQ - 1 + PLANE - 1 + NZ)

    def send_qkv(h, o):
        to = lax.rem(seq + o, NSEQ)
        for a, array in enumerate((prim, tang)):
            pltpu.make_async_remote_copy(
                array.at[:, :, head_columns(to, h)],
                qkv.at[h, :, rows_of(seq), pl.ds(a * 128, 128)],
                qkv_send.at[h],
                qkv_recv.at[h],
                device_id=(dp, to),
                device_id_type=MESH,
            ).start()

    def keep_qkv(h):
        for a, array in enumerate((prim, tang)):
            pltpu.make_async_copy(
                array.at[:, :, head_columns(seq, h)],
                qkv.at[h, :, rows_of(seq), pl.ds(a * 128, 128)],
                qkv_recv.at[h],
            ).start()

    place = c * 16 + (dp // 2) * 2 + yh

    def quarter(dp_to):
        return pl.ds(pl.multiple_of((dp_to // 8 * 2 + dp_to % 2) * QUARTER, 128), QUARTER)

    def send_cot(o):
        there = lax.rem(here + o, PLANE)
        pltpu.make_async_remote_copy(
            cot.at[:, quarter(there // 2)],
            cots.at[rows_of(place)],
            cot_send,
            cot_recv,
            device_id=(there // 2, z * 2 + there % 2),
            device_id_type=MESH,
        ).start()

    def first(o, carry):
        send_qkv(0, o)
        return carry

    def second(o, carry):
        send_qkv(1, o)
        send_cot(2 * o)
        send_cot(2 * o + 1)
        return carry

    keep_qkv(0)
    lax.fori_loop(1, NSEQ, first, 0)
    send_cot(1)
    lax.fori_loop(1, NSEQ, second, 0)
    keep_qkv(1)
    pltpu.make_async_copy(cot.at[:, quarter(dp)], cots.at[rows_of(place)], cot_recv).start()

    def attend(h, between):
        def one(step, carry):
            even = lax.rem(step, 2) == 0
            b = lax.rem(z + jnp.where(even, 4 - step // 2, 5 + step // 2), NZ)
            rows = pl.ds(pl.multiple_of(b * BLOCK, BLOCK), BLOCK)
            q = qkv[h, 0, rows, :]
            query, dquery = q[:, :HEAD_DIM], q[:, HEAD_DIM:]
            contract = (((1,), (1,)), ((), ()))
            scores = lax.dot_general(
                query, qkv[h, 1, :, :HEAD_DIM], contract, preferred_element_type=jnp.float32
            )
            dscores = lax.dot_general(
                jnp.concatenate([dquery, query], axis=1), qkv[h, 1], contract,
                preferred_element_type=jnp.float32,
            ) * SCALE
            top = jnp.max(scores, axis=-1, keepdims=True)
            expo = jnp.exp((scores - top) * SCALE)
            probs = expo * (1.0 / jnp.sum(expo, axis=-1, keepdims=True))
            centre = jnp.sum(probs * dscores, axis=-1, keepdims=True)
            dprobs = (probs * (dscores - centre)).astype(jnp.bfloat16)
            both = jnp.dot(
                probs.astype(jnp.bfloat16), qkv[h, 2], preferred_element_type=jnp.float32
            )
            dout = both[:, HEAD_DIM:] + jnp.dot(
                dprobs, qkv[h, 2, :, :HEAD_DIM], preferred_element_type=jnp.float32
            )
            own[h, rows, :] = both[:, :HEAD_DIM].astype(jnp.bfloat16)
            own_t[h, rows, :] = dout.astype(jnp.bfloat16)

            for source, target, recv in (
                (own, att_out, att_recv.at[h, seq]), (own_t, tan_out, tan_recv)
            ):
                for y in (0, 1):
                    to = b * 2 + y

                    @pl.when(to != seq)
                    def _():
                        pltpu.make_async_remote_copy(
                            source.at[h, rows_of(to)], target.at[:, head_columns(seq, h)],
                            out_send, recv, device_id=(dp, to), device_id_type=MESH,
                        ).start()

                    @pl.when(to == seq)
                    def _():
                        pltpu.make_async_copy(
                            source.at[h, rows_of(to)], target.at[:, head_columns(seq, h)], recv
                        ).start()

            for at, what in between:
                @pl.when(step == at)
                def _():
                    what()

            return carry

        lax.fori_loop(0, BLOCKS, one, 0)

    def spread(h):
        def one(o, carry):
            step = o // 2
            down = jnp.where(lax.rem(step, 2) == 0, 4 - step // 2, 5 + step // 2)
            source = lax.rem(z + NZ - down, NZ) * 2 + lax.rem(o, 2)
            offset = lax.rem(source // 2 - z + NZ, NZ)
            x_to, way = summed_at(offset), offset // 4
            wait_bytes(att_out.at[:, head_columns(source, h)], att_recv.at[h, source])
            lanes = pl.ds(pl.multiple_of(way * 128, 128), 128)
            for yl_to in (0, 1):
                dp_to = (yl_to * 4 + x_to) * 2 + c
                seq_to = z * 2 + source % 2
                is_here = jnp.logical_and(dp_to == dp, seq_to == seq)

                @pl.when(is_here)
                def _():
                    pltpu.make_async_copy(
                        att_out.at[:, head_columns(source, h)],
                        atts.at[h, rows_of(place), lanes], spread_recv.at[h],
                    ).start()

                @pl.when(jnp.logical_not(is_here))
                def _():
                    pltpu.make_async_remote_copy(
                        att_out.at[:, head_columns(source, h)],
                        atts.at[h, rows_of(place), lanes],
                        spread_send.at[h], spread_recv.at[h],
                        device_id=(dp_to, seq_to), device_id_type=MESH,
                    ).start()

            return carry

        lax.fori_loop(0, NSEQ, one, 0)

    def core_rows(core):
        return pl.ds(pl.multiple_of(core * (PLANE_TOKENS // 2), 128), PLANE_TOKENS // 2)

    def exchange(h):
        wait_bytes(atts.at[h, core_rows(c)], spread_recv.at[h])
        pltpu.make_async_remote_copy(
            atts.at[h, core_rows(c)], atts.at[h, core_rows(c)], core_send.at[h],
            core_recv.at[h], device_id=(dp + 1 - 2 * c, seq), device_id_type=MESH,
        ).start()

    def weigh(h):
        wait_bytes(atts.at[h, core_rows(1 - c)], core_recv.at[h])
        span = 1024

        def one(n, carry):
            tokens = pl.ds(pl.multiple_of(n * span, span), span)
            product = lax.dot_general(
                cots[tokens, :], atts[h, tokens, :], (((0,), (0,)), ((), ())),
                preferred_element_type=jnp.float32,
            )
            term[h] = jnp.where(n == 0, product, term[h] + product)
            return carry

        lax.fori_loop(0, PLANE_TOKENS // span, one, 0)

        def send(n, carry):
            block = pl.ds(pl.multiple_of(n * ROWS, ROWS), ROWS)
            dp_to = (yl * 4 + 2 * c + n // 2) * 2 + n % 2
            for way in (0, 1):
                seq_to = lax.rem(z + columns_at(x, way), NZ) * 2 + yh
                source = term.at[h, block, pl.ds(way * 128, 128)]

                def away():
                    pltpu.make_async_remote_copy(
                        source, terms.at[h, z], term_send.at[h], term_recv.at[h],
                        device_id=(dp_to, seq_to), device_id_type=MESH,
                    ).start()

                if way:
                    away()
                else:
                    is_mine = jnp.logical_and(mine, n == 0)
                    pl.when(jnp.logical_not(is_mine))(away)

                    @pl.when(is_mine)
                    def _():
                        pltpu.make_async_copy(source, terms.at[h, z], term_recv.at[h]).start()

            return carry

        lax.fori_loop(0, 4, send, 0)

    def total(h):
        wait_bytes(terms.at[h], term_recv.at[h])
        result = terms[h, 0]
        for s in range(1, NZ):
            result = result + terms[h, s]
        wg_out[:, pl.ds(h * 128, 128)] = result

    wait_bytes(qkv.at[0], qkv_recv.at[0])
    attend(0, ())
    wait_bytes(qkv.at[1], qkv_recv.at[1])
    attend(1, ((4, lambda: spread(0)), (6, lambda: exchange(0))))
    spread(1)
    wait_bytes(cots, cot_recv)
    weigh(0)
    exchange(1)
    weigh(1)
    total(0)
    total(1)

    wait_bytes(tan_out, tan_recv)
    sent = pl.ds(0, (NSEQ - 1) * TOKENS)
    wait_bytes(cots.at[pl.ds(0, (PLANE - 1) * TOKENS)], cot_send)
    for h in range(LOCAL_HEADS):
        wait_bytes(qkv.at[h, :, sent], qkv_send.at[h])
        wait_bytes(atts.at[h, pl.ds(0, 15 * TOKENS)], spread_send.at[h])
        wait_bytes(atts.at[h, core_rows(c)], core_send.at[h])

        @pl.when(mine)
        def _():
            wait_bytes(terms.at[h, pl.ds(0, NZ - 1)], term_send.at[h])

        @pl.when(jnp.logical_not(mine))
        def _():
            wait_bytes(terms.at[h], term_send.at[h])

    wait_bytes(qkv.at[:, 0, sent], out_send)


def body(primal, tangent, cotangent):
    prim = jnp.transpose(primal[0], (1, 0, 2))
    tang = jnp.transpose(tangent[0], (1, 0, 2))
    hbm = pl.BlockSpec(memory_space=pl.ANY)
    dma = pltpu.SemaphoreType.DMA
    bf16, f32 = jnp.bfloat16, jnp.float32
    att, tan, wg = pl.pallas_call(
        kernel,
        out_shape=(
            jax.ShapeDtypeStruct((TOKENS, WIDTH), bf16),
            jax.ShapeDtypeStruct((TOKENS, WIDTH), bf16),
            jax.ShapeDtypeStruct((ROWS, 256), f32),
        ),
        in_specs=[hbm] * 3,
        out_specs=(hbm, hbm, pl.BlockSpec(memory_space=pltpu.VMEM)),
        scratch_shapes=[
            pltpu.VMEM((LOCAL_HEADS, 3, SEQ_LEN, 256), bf16),
            pltpu.VMEM((PLANE_TOKENS, QUARTER), bf16),
            pltpu.VMEM((LOCAL_HEADS, SEQ_LEN, HEAD_DIM), bf16),
            pltpu.VMEM((LOCAL_HEADS, SEQ_LEN, HEAD_DIM), bf16),
            pltpu.VMEM((LOCAL_HEADS, PLANE_TOKENS, 256), bf16),
            pltpu.VMEM((LOCAL_HEADS, QUARTER, 256), f32),
            pltpu.VMEM((LOCAL_HEADS, NZ, ROWS, HEAD_DIM), f32),
            dma((2,)), dma((2,)), dma(()), dma(()), dma(()), dma((2, NSEQ)), dma(()),
            dma((2,)), dma((2,)), dma((2,)), dma((2,)), dma((2,)), dma((2,)),
        ],
        compiler_params=pltpu.CompilerParams(
            collective_id=0, has_side_effects=True, vmem_limit_bytes=56 * 2**20
        ),
        cost_estimate=pl.CostEstimate(
            flops=2 * 2 * SEQ_LEN * SEQ_LEN * 128 * 6 + 2 * FEATURES * 256 * SEQ_LEN,
            bytes_accessed=16 * 2**20, transcendentals=2 * SEQ_LEN * SEQ_LEN,
        ),
        name="attention_jvp",
    )(prim, tang, cotangent[0])
    return att[None], tan[None], wg


def solution(mesh):
    return jax.shard_map(
        body,
        mesh=mesh,
        in_specs=(P("dp", "seq", None, None), P("dp", "seq", None, None), P("dp", "seq", None)),
        out_specs=(P("dp", "seq", None), P("dp", "seq", None), P("dp", "seq")),
        check_vma=False,
    )
```

```python
import jax
import jax.numpy as jnp
from jax import lax
from jax.experimental import pallas as pl
from jax.experimental.pallas import tpu as pltpu
from jax.sharding import PartitionSpec as P

MESH = pl.DeviceIdType.MESH
HEAD_DIM = 128
TOKENS = 128
SEQ_LEN = 2048
WIDTH = 4096
FEATURES = 2560
QUARTER = FEATURES // 4
ROWS = 160
NSEQ = 16
NDP = 16
PLANE = 32
PLANE_TOKENS = PLANE * TOKENS
NZ = 8
LOCAL_HEADS = 2
BLOCK = 256
BLOCKS = SEQ_LEN // BLOCK
SCALE = 1.0 / HEAD_DIM**0.5


def wait_bytes(ref, sem):
    pltpu.make_async_copy(ref, ref, sem).wait()


def kernel(
    prim, tang, cot, att_out, tan_out, wg_out,
    qkv, cots, own, own_t, stats, atts, total_of, term, terms,
    qkv_send, qkv_recv, cot_send, cot_recv, out_send, att_recv, tan_recv,
    spread_send, spread_recv, core_send, core_recv, term_send, term_recv,
):
    dp, seq = lax.axis_index("dp"), lax.axis_index("seq")
    z, yh = seq // 2, seq % 2
    yl, x, c = dp // 8, (dp // 2) % 4, dp % 2
    here = dp * 2 + yh
    mine = jnp.logical_and(x == 0, c == 0)

    def columns_at(x_at, way):
        apart = jnp.where(x_at == 0, 4, NZ - x_at)
        return jnp.where(way == 0, x_at, apart)

    def summed_at(offset):
        near = jnp.where(offset > 4, NZ - offset, offset)
        return lax.rem(near, 4)

    def rows_of(device):
        return pl.ds(pl.multiple_of(device * TOKENS, TOKENS), TOKENS)

    def head_columns(device, h):
        return pl.ds(pl.multiple_of(device * 256 + h * 128, 128), 128)

    barrier = pltpu.get_barrier_semaphore()

    def greet(dp_to, seq_to):
        pl.semaphore_signal(barrier, inc=1, device_id=(dp_to, seq_to), device_id_type=MESH)

    def greet_clip(o, carry):
        greet(dp, lax.rem(seq + o, NSEQ))
        return carry

    def greet_plane(o, carry):
        there = lax.rem(here + o, PLANE)
        greet(there // 2, z * 2 + there % 2)
        return carry

    def greet_terms(o, carry):
        source_dp = (yl * 4 + summed_at(o)) * 2 + x // 2

        @pl.when(jnp.logical_not(jnp.logical_and(mine, o == 0)))
        def _():
            greet(source_dp, lax.rem(z + NZ - o, NZ) * 2 + yh)

        return carry

    lax.fori_loop(1, NSEQ, greet_clip, 0)
    lax.fori_loop(1, PLANE, greet_plane, 0)
    lax.fori_loop(0, NZ, greet_terms, 0)

    @pl.when(mine)
    def _():
        pl.semaphore_wait(barrier, NSEQ - 1 + PLANE - 1 + NZ - 1)

    @pl.when(jnp.logical_not(mine))
    def _():
        pl.semaphore_wait(barrier, NSEQ - 1 + PLANE - 1 + NZ)

    def send_qkv(h, o):
        to = lax.rem(seq + o, NSEQ)
        for a, array in enumerate((prim, tang)):
            pltpu.make_async_remote_copy(
                array.at[:, :, head_columns(to, h)],
                qkv.at[h, :, rows_of(seq), pl.ds(a * 128, 128)],
                qkv_send.at[h],
                qkv_recv.at[h],
                device_id=(dp, to),
                device_id_type=MESH,
            ).start()

    def keep_qkv(h):
        for a, array in enumerate((prim, tang)):
            pltpu.make_async_copy(
                array.at[:, :, head_columns(seq, h)],
                qkv.at[h, :, rows_of(seq), pl.ds(a * 128, 128)],
                qkv_recv.at[h],
            ).start()

    place = x * 8 + yh * 4 + yl * 2 + c

    def quarter(dp_to):
        return pl.ds(pl.multiple_of((dp_to // 8 * 2 + dp_to % 2) * QUARTER, 128), QUARTER)

    def tokens_at(first, places):
        return pl.ds(pl.multiple_of(first * TOKENS, TOKENS), places * TOKENS)

    same_y, same_x = tokens_at(x * 8 + yh * 4, 4), tokens_at(x * 8, 8)

    def cot_quarters():
        for n in range(1, 4):
            dp_to = (lax.rem(yl + n // 2, 2) * 4 + x) * 2 + lax.rem(c + n % 2, 2)
            pltpu.make_async_remote_copy(
                cot.at[:, quarter(dp_to)], cots.at[rows_of(place)],
                cot_send.at[n - 1], cot_recv.at[n - 1],
                device_id=(dp_to, seq), device_id_type=MESH,
            ).start()
        pltpu.make_async_copy(
            cot.at[:, quarter(dp)], cots.at[rows_of(place)], cot_recv.at[3]
        ).start()

    def cot_along_y():
        for n in range(4):
            wait_bytes(cots.at[rows_of(place)], cot_recv.at[n])
        pltpu.make_async_remote_copy(
            cots.at[same_y], cots.at[same_y], cot_send.at[3], cot_recv.at[4],
            device_id=(dp, z * 2 + 1 - yh), device_id_type=MESH,
        ).start()

    def cot_along_x():
        wait_bytes(cots.at[same_y], cot_recv.at[4])
        for n in range(1, 4):
            dp_to = (yl * 4 + lax.rem(x + n, 4)) * 2 + c
            pltpu.make_async_remote_copy(
                cots.at[same_x], cots.at[same_x], cot_send.at[3 + n], cot_recv.at[4 + n],
                device_id=(dp_to, seq), device_id_type=MESH,
            ).start()

    def first(o, carry):
        send_qkv(0, o)
        return carry

    def second(o, carry):
        send_qkv(1, o)
        return carry

    cot_quarters()
    keep_qkv(0)
    lax.fori_loop(1, NSEQ, first, 0)
    cot_along_y()
    lax.fori_loop(1, NSEQ, second, 0)
    keep_qkv(1)
    cot_along_x()

    contract = (((1,), (1,)), ((), ()))

    def block_at(step):
        even = lax.rem(step, 2) == 0
        return lax.rem(z + jnp.where(even, 4 - step // 2, 5 + step // 2), NZ)

    def rows_at(step):
        return pl.ds(pl.multiple_of(block_at(step) * BLOCK, BLOCK), BLOCK)

    def scores_of(h, rows):
        return lax.dot_general(
            qkv[h, 0, rows, :HEAD_DIM], qkv[h, 1, :, :HEAD_DIM], contract,
            preferred_element_type=jnp.float32,
        )

    def dprobs_of(h, rows, probs):
        q = qkv[h, 0, rows, :]
        dscores = lax.dot_general(
            jnp.concatenate([q[:, HEAD_DIM:], q[:, :HEAD_DIM]], axis=1), qkv[h, 1], contract,
            preferred_element_type=jnp.float32,
        ) * SCALE
        centre = jnp.sum(probs * dscores, axis=-1, keepdims=True)
        return (probs * (dscores - centre)).astype(jnp.bfloat16)

    def go_home(source, target, recv, h, step):
        for y in (0, 1):
            to = block_at(step) * 2 + y

            @pl.when(to != seq)
            def _():
                pltpu.make_async_remote_copy(
                    source.at[h, rows_of(to)], target.at[:, head_columns(seq, h)],
                    out_send, recv, device_id=(dp, to), device_id_type=MESH,
                ).start()

            @pl.when(to == seq)
            def _():
                pltpu.make_async_copy(
                    source.at[h, rows_of(to)], target.at[:, head_columns(seq, h)], recv
                ).start()

    def primal_home(h, step):
        go_home(own, att_out, att_recv.at[h, seq], h, step)

    def tangent_home(h, step):
        go_home(own_t, tan_out, tan_recv, h, step)

    def attend(h, step):
        rows = rows_at(step)
        scores = scores_of(h, rows)
        top = jnp.max(scores, axis=-1, keepdims=True)
        expo = jnp.exp((scores - top) * SCALE)
        probs = expo * (1.0 / jnp.sum(expo, axis=-1, keepdims=True))
        dprobs = dprobs_of(h, rows, probs)
        both = jnp.dot(
            probs.astype(jnp.bfloat16), qkv[h, 2], preferred_element_type=jnp.float32
        )
        dout = both[:, HEAD_DIM:] + jnp.dot(
            dprobs, qkv[h, 2, :, :HEAD_DIM], preferred_element_type=jnp.float32
        )
        own[h, rows, :] = both[:, :HEAD_DIM].astype(jnp.bfloat16)
        own_t[h, rows, :] = dout.astype(jnp.bfloat16)

    def attend_primal(h, step):
        rows = rows_at(step)
        scores = scores_of(h, rows)
        top = jnp.max(scores, axis=-1, keepdims=True)
        expo = jnp.exp((scores - top) * SCALE)
        share = 1.0 / jnp.sum(expo, axis=-1, keepdims=True)
        out = jnp.dot(
            (expo * share).astype(jnp.bfloat16), qkv[h, 2, :, :HEAD_DIM],
            preferred_element_type=jnp.float32,
        )
        own[h, rows, :] = out.astype(jnp.bfloat16)
        stats[rows, 0:1] = top
        stats[rows, 1:2] = share

    def attend_tangent(h, step):
        rows = rows_at(step)
        probs = jnp.exp((scores_of(h, rows) - stats[rows, 0:1]) * SCALE) * stats[rows, 1:2]
        dprobs = dprobs_of(h, rows, probs)
        dout = jnp.dot(
            probs.astype(jnp.bfloat16), qkv[h, 2, :, HEAD_DIM:],
            preferred_element_type=jnp.float32,
        ) + jnp.dot(dprobs, qkv[h, 2, :, :HEAD_DIM], preferred_element_type=jnp.float32)
        own_t[h, rows, :] = dout.astype(jnp.bfloat16)

    def steps(h, start, stop, *parts):
        def one(step, carry):
            for part in parts:
                part(h, step)
            return carry

        lax.fori_loop(start, stop, one, 0)

    def spread(h):
        def one(o, carry):
            step = o // 2
            down = jnp.where(lax.rem(step, 2) == 0, 4 - step // 2, 5 + step // 2)
            source = lax.rem(z + NZ - down, NZ) * 2 + lax.rem(o, 2)
            offset = lax.rem(source // 2 - z + NZ, NZ)
            x_to, way = summed_at(offset), offset // 4
            wait_bytes(att_out.at[:, head_columns(source, h)], att_recv.at[h, source])
            lanes = pl.ds(pl.multiple_of(way * 128, 128), 128)
            for yl_to in (0, 1):
                dp_to = (yl_to * 4 + x_to) * 2 + c
                seq_to = z * 2 + source % 2
                is_here = jnp.logical_and(dp_to == dp, seq_to == seq)

                @pl.when(is_here)
                def _():
                    pltpu.make_async_copy(
                        att_out.at[:, head_columns(source, h)],
                        atts.at[h, place // 2, c, :, lanes], spread_recv.at[h],
                    ).start()

                @pl.when(jnp.logical_not(is_here))
                def _():
                    pltpu.make_async_remote_copy(
                        att_out.at[:, head_columns(source, h)],
                        atts.at[h, place // 2, c, :, lanes],
                        spread_send.at[h], spread_recv.at[h],
                        device_id=(dp_to, seq_to), device_id_type=MESH,
                    ).start()

            return carry

        lax.fori_loop(0, NSEQ, one, 0)

    def exchange(h):
        wait_bytes(atts.at[h, :, c], spread_recv.at[h])
        pltpu.make_async_remote_copy(
            atts.at[h, :, c], atts.at[h, :, c], core_send.at[h],
            core_recv.at[h], device_id=(dp + 1 - 2 * c, seq), device_id_type=MESH,
        ).start()

    def weigh(h):
        wait_bytes(atts.at[h, :, 1 - c], core_recv.at[h])
        span = 1024

        def one(n, carry):
            tokens = pl.ds(pl.multiple_of(n * span, span), span)
            product = lax.dot_general(
                cots[tokens, :], atts[h, pl.ds(n * 4, 4)].reshape(span, 256), (((0,), (0,)), ((), ())),
                preferred_element_type=jnp.float32,
            )
            total = jnp.where(n == 0, product, total_of[...] + product)
            total_of[...] = total
            term[h] = total.astype(jnp.bfloat16)
            return carry

        lax.fori_loop(0, PLANE_TOKENS // span, one, 0)

        def send(n, carry):
            block = pl.ds(pl.multiple_of(n * ROWS, ROWS), ROWS)
            dp_to = (yl * 4 + 2 * c + n // 2) * 2 + n % 2
            for way in (0, 1):
                seq_to = lax.rem(z + columns_at(x, way), NZ) * 2 + yh
                source = term.at[h, block, pl.ds(way * 128, 128)]

                def away():
                    pltpu.make_async_remote_copy(
                        source, terms.at[h, z], term_send.at[h], term_recv.at[h],
                        device_id=(dp_to, seq_to), device_id_type=MESH,
                    ).start()

                if way:
                    away()
                else:
                    is_mine = jnp.logical_and(mine, n == 0)
                    pl.when(jnp.logical_not(is_mine))(away)

                    @pl.when(is_mine)
                    def _():
                        pltpu.make_async_copy(source, terms.at[h, z], term_recv.at[h]).start()

            return carry

        lax.fori_loop(0, 4, send, 0)

    def total(h):
        wait_bytes(terms.at[h], term_recv.at[h])
        result = terms[h, 0].astype(jnp.float32)
        for s in range(1, NZ):
            result = result + terms[h, s].astype(jnp.float32)
        wg_out[:, pl.ds(h * 128, 128)] = result

    wait_bytes(qkv.at[0], qkv_recv.at[0])
    steps(0, 0, BLOCKS, attend, primal_home)
    wait_bytes(qkv.at[1], qkv_recv.at[1])
    steps(0, 0, BLOCKS, tangent_home)
    steps(1, 0, BLOCKS, attend_primal, primal_home)
    spread(0)
    steps(1, 0, 3, attend_tangent, tangent_home)
    exchange(0)
    spread(1)
    steps(1, 3, 6, attend_tangent, tangent_home)
    for n in range(3):
        wait_bytes(cots.at[same_x], cot_recv.at[5 + n])
    weigh(0)
    exchange(1)
    steps(1, 6, BLOCKS, attend_tangent, tangent_home)
    weigh(1)
    total(0)
    total(1)

    wait_bytes(tan_out, tan_recv)
    sent = pl.ds(0, (NSEQ - 1) * TOKENS)
    for n in range(3):
        wait_bytes(cots.at[rows_of(place)], cot_send.at[n])
        wait_bytes(cots.at[same_x], cot_send.at[4 + n])
    wait_bytes(cots.at[same_y], cot_send.at[3])
    for h in range(LOCAL_HEADS):
        wait_bytes(qkv.at[h, :, sent], qkv_send.at[h])
        wait_bytes(atts.at[h, pl.ds(0, 15), c], spread_send.at[h])
        wait_bytes(atts.at[h, :, c], core_send.at[h])

        @pl.when(mine)
        def _():
            wait_bytes(terms.at[h, pl.ds(0, NZ - 1)], term_send.at[h])

        @pl.when(jnp.logical_not(mine))
        def _():
            wait_bytes(terms.at[h], term_send.at[h])

    wait_bytes(qkv.at[:, 0, sent], out_send)


def body(primal, tangent, cotangent):
    prim = jnp.transpose(primal[0], (1, 0, 2))
    tang = jnp.transpose(tangent[0], (1, 0, 2))
    hbm = pl.BlockSpec(memory_space=pl.ANY)
    dma = pltpu.SemaphoreType.DMA
    bf16, f32 = jnp.bfloat16, jnp.float32
    att, tan, wg = pl.pallas_call(
        kernel,
        out_shape=(
            jax.ShapeDtypeStruct((TOKENS, WIDTH), bf16),
            jax.ShapeDtypeStruct((TOKENS, WIDTH), bf16),
            jax.ShapeDtypeStruct((ROWS, 256), f32),
        ),
        in_specs=[hbm] * 3,
        out_specs=(hbm, hbm, pl.BlockSpec(memory_space=pltpu.VMEM)),
        scratch_shapes=[
            pltpu.VMEM((LOCAL_HEADS, 3, SEQ_LEN, 256), bf16),
            pltpu.VMEM((PLANE_TOKENS, QUARTER), bf16),
            pltpu.VMEM((LOCAL_HEADS, SEQ_LEN, HEAD_DIM), bf16),
            pltpu.VMEM((LOCAL_HEADS, SEQ_LEN, HEAD_DIM), bf16),
            pltpu.VMEM((SEQ_LEN, HEAD_DIM), f32),
            pltpu.VMEM((LOCAL_HEADS, PLANE // 2, 2, TOKENS, 256), bf16),
            pltpu.VMEM((QUARTER, 256), f32),
            pltpu.VMEM((LOCAL_HEADS, QUARTER, 256), bf16),
            pltpu.VMEM((LOCAL_HEADS, NZ, ROWS, HEAD_DIM), bf16),
            dma((2,)), dma((2,)), dma((7,)), dma((8,)), dma(()), dma((2, NSEQ)), dma(()),
            dma((2,)), dma((2,)), dma((2,)), dma((2,)), dma((2,)), dma((2,)),
        ],
        compiler_params=pltpu.CompilerParams(
            collective_id=0, has_side_effects=True, vmem_limit_bytes=56 * 2**20
        ),
        cost_estimate=pl.CostEstimate(
            flops=2 * 2 * SEQ_LEN * SEQ_LEN * 128 * 6 + 2 * FEATURES * 256 * SEQ_LEN,
            bytes_accessed=16 * 2**20, transcendentals=2 * SEQ_LEN * SEQ_LEN,
        ),
        name="attention_jvp",
    )(prim, tang, cotangent[0])
    return att[None], tan[None], wg


def solution(mesh):
    return jax.shard_map(
        body,
        mesh=mesh,
        in_specs=(P("dp", "seq", None, None), P("dp", "seq", None, None), P("dp", "seq", None)),
        out_specs=(P("dp", "seq", None), P("dp", "seq", None), P("dp", "seq")),
        check_vma=False,
    )
```

```python
import jax
import jax.numpy as jnp
from jax import lax
from jax.experimental import pallas as pl
from jax.experimental.pallas import tpu as pltpu
from jax.sharding import PartitionSpec as P

MESH = pl.DeviceIdType.MESH
HEAD_DIM = 128
TOKENS = 128
SEQ_LEN = 2048
WIDTH = 4096
FEATURES = 2560
QUARTER = FEATURES // 4
ROWS = 160
NSEQ = 16
NDP = 16
PLANE = 32
PLANE_TOKENS = PLANE * TOKENS
NZ = 8
LOCAL_HEADS = 2
BLOCK = 256
BLOCKS = SEQ_LEN // BLOCK
SCALE = 1.0 / HEAD_DIM**0.5


def wait_bytes(ref, sem):
    pltpu.make_async_copy(ref, ref, sem).wait()


def kernel(
    prim, tang, cot, att_out, tan_out, wg_out,
    qkv, cots, own, own_t, stats, atts, total_of, term, terms,
    qkv_send, qkv_recv, cot_send, cot_recv, out_send, att_recv, tan_recv,
    spread_send, spread_recv, core_send, core_recv, term_send, term_recv,
):
    dp, seq = lax.axis_index("dp"), lax.axis_index("seq")
    z, yh = seq // 2, seq % 2
    yl, x, c = dp // 8, (dp // 2) % 4, dp % 2
    here = dp * 2 + yh
    mine = jnp.logical_and(x == 0, c == 0)

    def columns_at(x_at, way):
        apart = jnp.where(x_at == 0, 4, NZ - x_at)
        return jnp.where(way == 0, x_at, apart)

    def summed_at(offset):
        near = jnp.where(offset > 4, NZ - offset, offset)
        return lax.rem(near, 4)

    def rows_of(device):
        return pl.ds(pl.multiple_of(device * TOKENS, TOKENS), TOKENS)

    def head_columns(device, h):
        return pl.ds(pl.multiple_of(device * 256 + h * 128, 128), 128)

    barrier = pltpu.get_barrier_semaphore()

    def greet(dp_to, seq_to):
        pl.semaphore_signal(barrier, inc=1, device_id=(dp_to, seq_to), device_id_type=MESH)

    def greet_clip(o, carry):
        greet(dp, lax.rem(seq + o, NSEQ))
        return carry

    def greet_plane(o, carry):
        there = lax.rem(here + o, PLANE)
        greet(there // 2, z * 2 + there % 2)
        return carry

    def greet_terms(o, carry):
        source_dp = (yl * 4 + summed_at(o)) * 2 + x // 2

        @pl.when(jnp.logical_not(jnp.logical_and(mine, o == 0)))
        def _():
            greet(source_dp, lax.rem(z + NZ - o, NZ) * 2 + yh)

        return carry

    lax.fori_loop(1, NSEQ, greet_clip, 0)
    lax.fori_loop(1, PLANE, greet_plane, 0)
    lax.fori_loop(0, NZ, greet_terms, 0)

    @pl.when(mine)
    def _():
        pl.semaphore_wait(barrier, NSEQ - 1 + PLANE - 1 + NZ - 1)

    @pl.when(jnp.logical_not(mine))
    def _():
        pl.semaphore_wait(barrier, NSEQ - 1 + PLANE - 1 + NZ)

    def send_qkv(h, o):
        to = lax.rem(seq + o, NSEQ)
        for a, array in enumerate((prim, tang)):
            pltpu.make_async_remote_copy(
                array.at[:, :, head_columns(to, h)],
                qkv.at[h, :, rows_of(seq), pl.ds(a * 128, 128)],
                qkv_send.at[h],
                qkv_recv.at[h],
                device_id=(dp, to),
                device_id_type=MESH,
            ).start()

    def keep_qkv(h):
        for a, array in enumerate((prim, tang)):
            pltpu.make_async_copy(
                array.at[:, :, head_columns(seq, h)],
                qkv.at[h, :, rows_of(seq), pl.ds(a * 128, 128)],
                qkv_recv.at[h],
            ).start()

    place = x * 8 + yh * 4 + yl * 2 + c

    def quarter(dp_to):
        return pl.ds(pl.multiple_of((dp_to // 8 * 2 + dp_to % 2) * QUARTER, 128), QUARTER)

    def tokens_at(first, places):
        return pl.ds(pl.multiple_of(first * TOKENS, TOKENS), places * TOKENS)

    same_y, same_x = tokens_at(x * 8 + yh * 4, 4), tokens_at(x * 8, 8)

    def cot_quarters():
        for n in range(1, 4):
            dp_to = (lax.rem(yl + n // 2, 2) * 4 + x) * 2 + lax.rem(c + n % 2, 2)
            pltpu.make_async_remote_copy(
                cot.at[:, quarter(dp_to)], cots.at[rows_of(place)],
                cot_send.at[n - 1], cot_recv.at[n - 1],
                device_id=(dp_to, seq), device_id_type=MESH,
            ).start()
        pltpu.make_async_copy(
            cot.at[:, quarter(dp)], cots.at[rows_of(place)], cot_recv.at[3]
        ).start()

    def cot_along_y():
        for n in range(4):
            wait_bytes(cots.at[rows_of(place)], cot_recv.at[n])
        pltpu.make_async_remote_copy(
            cots.at[same_y], cots.at[same_y], cot_send.at[3], cot_recv.at[4],
            device_id=(dp, z * 2 + 1 - yh), device_id_type=MESH,
        ).start()

    def cot_along_x():
        wait_bytes(cots.at[same_y], cot_recv.at[4])
        for n in range(1, 4):
            dp_to = (yl * 4 + lax.rem(x + n, 4)) * 2 + c
            pltpu.make_async_remote_copy(
                cots.at[same_x], cots.at[same_x], cot_send.at[3 + n], cot_recv.at[4 + n],
                device_id=(dp_to, seq), device_id_type=MESH,
            ).start()

    def first(o, carry):
        send_qkv(0, o)
        return carry

    def second(o, carry):
        send_qkv(1, o)
        return carry

    cot_quarters()
    keep_qkv(0)
    lax.fori_loop(1, NSEQ, first, 0)
    cot_along_y()
    lax.fori_loop(1, NSEQ, second, 0)
    keep_qkv(1)
    cot_along_x()

    contract = (((1,), (1,)), ((), ()))

    def block_at(step):
        even = lax.rem(step, 2) == 0
        return lax.rem(z + jnp.where(even, 4 - step // 2, 5 + step // 2), NZ)

    def rows_at(step):
        return pl.ds(pl.multiple_of(block_at(step) * BLOCK, BLOCK), BLOCK)

    def scores_of(h, rows):
        return lax.dot_general(
            qkv[h, 0, rows, :HEAD_DIM], qkv[h, 1, :, :HEAD_DIM], contract,
            preferred_element_type=jnp.float32,
        )

    def dprobs_of(h, rows, probs):
        q = qkv[h, 0, rows, :]
        dscores = lax.dot_general(
            jnp.concatenate([q[:, HEAD_DIM:], q[:, :HEAD_DIM]], axis=1), qkv[h, 1], contract,
            preferred_element_type=jnp.float32,
        ) * SCALE
        centre = jnp.sum(probs * dscores, axis=-1, keepdims=True)
        return (probs * (dscores - centre)).astype(jnp.bfloat16)

    def go_home(source, target, recv, h, step):
        for y in (0, 1):
            to = block_at(step) * 2 + y

            @pl.when(to != seq)
            def _():
                pltpu.make_async_remote_copy(
                    source.at[h, rows_of(to)], target.at[:, head_columns(seq, h)],
                    out_send, recv, device_id=(dp, to), device_id_type=MESH,
                ).start()

            @pl.when(to == seq)
            def _():
                pltpu.make_async_copy(
                    source.at[h, rows_of(to)], target.at[:, head_columns(seq, h)], recv
                ).start()

    def primal_home(h, step):
        go_home(own, att_out, att_recv.at[h, seq], h, step)

    def tangent_home(h, step):
        go_home(own_t, tan_out, tan_recv, h, step)

    def attend(h, step):
        rows = rows_at(step)
        scores = scores_of(h, rows)
        top = jnp.max(scores, axis=-1, keepdims=True)
        expo = jnp.exp((scores - top) * SCALE)
        probs = expo * (1.0 / jnp.sum(expo, axis=-1, keepdims=True))
        dprobs = dprobs_of(h, rows, probs)
        both = jnp.dot(
            probs.astype(jnp.bfloat16), qkv[h, 2], preferred_element_type=jnp.float32
        )
        dout = both[:, HEAD_DIM:] + jnp.dot(
            dprobs, qkv[h, 2, :, :HEAD_DIM], preferred_element_type=jnp.float32
        )
        own[h, rows, :] = both[:, :HEAD_DIM].astype(jnp.bfloat16)
        own_t[h, rows, :] = dout.astype(jnp.bfloat16)

    def attend_primal(h, step):
        rows = rows_at(step)
        scores = scores_of(h, rows)
        top = jnp.max(scores, axis=-1, keepdims=True)
        expo = jnp.exp((scores - top) * SCALE)
        share = 1.0 / jnp.sum(expo, axis=-1, keepdims=True)
        out = jnp.dot(
            (expo * share).astype(jnp.bfloat16), qkv[h, 2, :, :HEAD_DIM],
            preferred_element_type=jnp.float32,
        )
        own[h, rows, :] = out.astype(jnp.bfloat16)
        stats[rows, 0:1] = top
        stats[rows, 1:2] = share

    def attend_tangent(h, step):
        rows = rows_at(step)
        probs = jnp.exp((scores_of(h, rows) - stats[rows, 0:1]) * SCALE) * stats[rows, 1:2]
        dprobs = dprobs_of(h, rows, probs)
        dout = jnp.dot(
            probs.astype(jnp.bfloat16), qkv[h, 2, :, HEAD_DIM:],
            preferred_element_type=jnp.float32,
        ) + jnp.dot(dprobs, qkv[h, 2, :, :HEAD_DIM], preferred_element_type=jnp.float32)
        own_t[h, rows, :] = dout.astype(jnp.bfloat16)

    def steps(h, start, stop, *parts):
        def one(step, carry):
            for part in parts:
                part(h, step)
            return carry

        lax.fori_loop(start, stop, one, 0)

    def spread(h):
        def one(o, carry):
            step = o // 2
            down = jnp.where(lax.rem(step, 2) == 0, 4 - step // 2, 5 + step // 2)
            source = lax.rem(z + NZ - down, NZ) * 2 + lax.rem(o, 2)
            offset = lax.rem(source // 2 - z + NZ, NZ)
            x_to, way = summed_at(offset), offset // 4
            wait_bytes(att_out.at[:, head_columns(source, h)], att_recv.at[h, source])
            lanes = pl.ds(pl.multiple_of(way * 128, 128), 128)
            for yl_to in (0, 1):
                dp_to = (yl_to * 4 + x_to) * 2 + c
                seq_to = z * 2 + source % 2
                is_here = jnp.logical_and(dp_to == dp, seq_to == seq)

                @pl.when(is_here)
                def _():
                    pltpu.make_async_copy(
                        att_out.at[:, head_columns(source, h)],
                        atts.at[h, place // 2, c, :, lanes], spread_recv.at[h],
                    ).start()

                @pl.when(jnp.logical_not(is_here))
                def _():
                    pltpu.make_async_remote_copy(
                        att_out.at[:, head_columns(source, h)],
                        atts.at[h, place // 2, c, :, lanes],
                        spread_send.at[h], spread_recv.at[h],
                        device_id=(dp_to, seq_to), device_id_type=MESH,
                    ).start()

            return carry

        lax.fori_loop(0, NSEQ, one, 0)

    def exchange(h):
        wait_bytes(atts.at[h, :, c], spread_recv.at[h])
        pltpu.make_async_remote_copy(
            atts.at[h, :, c], atts.at[h, :, c], core_send.at[h],
            core_recv.at[h], device_id=(dp + 1 - 2 * c, seq), device_id_type=MESH,
        ).start()

    def weigh(h):
        wait_bytes(atts.at[h, :, 1 - c], core_recv.at[h])
        span = 1024

        def one(n, carry):
            tokens = pl.ds(pl.multiple_of(n * span, span), span)
            product = lax.dot_general(
                cots[tokens, :], atts[h, pl.ds(n * 4, 4)].reshape(span, 256), (((0,), (0,)), ((), ())),
                preferred_element_type=jnp.float32,
            )
            total = jnp.where(n == 0, product, total_of[...] + product)
            total_of[...] = total
            term[h] = total.astype(jnp.bfloat16)
            return carry

        lax.fori_loop(0, PLANE_TOKENS // span, one, 0)

        def send(n, carry):
            block = pl.ds(pl.multiple_of(n * ROWS, ROWS), ROWS)
            dp_to = (yl * 4 + 2 * c + n // 2) * 2 + n % 2
            for way in (0, 1):
                seq_to = lax.rem(z + columns_at(x, way), NZ) * 2 + yh
                source = term.at[h, block, pl.ds(way * 128, 128)]

                def away():
                    pltpu.make_async_remote_copy(
                        source, terms.at[h, z], term_send.at[h], term_recv.at[h],
                        device_id=(dp_to, seq_to), device_id_type=MESH,
                    ).start()

                if way:
                    away()
                else:
                    is_mine = jnp.logical_and(mine, n == 0)
                    pl.when(jnp.logical_not(is_mine))(away)

                    @pl.when(is_mine)
                    def _():
                        pltpu.make_async_copy(source, terms.at[h, z], term_recv.at[h]).start()

            return carry

        lax.fori_loop(0, 4, send, 0)

    def total(h):
        wait_bytes(terms.at[h], term_recv.at[h])
        result = terms[h, 0].astype(jnp.float32)
        for s in range(1, NZ):
            result = result + terms[h, s].astype(jnp.float32)
        wg_out[:, pl.ds(h * 128, 128)] = result

    wait_bytes(qkv.at[0], qkv_recv.at[0])
    steps(0, 0, BLOCKS, attend, primal_home, tangent_home)
    wait_bytes(qkv.at[1], qkv_recv.at[1])
    steps(1, 0, BLOCKS, attend_primal, primal_home)
    spread(0)
    steps(1, 0, 3, attend_tangent, tangent_home)
    exchange(0)
    spread(1)
    steps(1, 3, 6, attend_tangent, tangent_home)
    for n in range(3):
        wait_bytes(cots.at[same_x], cot_recv.at[5 + n])
    weigh(0)
    exchange(1)
    steps(1, 6, BLOCKS, attend_tangent, tangent_home)
    weigh(1)
    total(0)
    total(1)

    wait_bytes(tan_out, tan_recv)
    sent = pl.ds(0, (NSEQ - 1) * TOKENS)
    for n in range(3):
        wait_bytes(cots.at[rows_of(place)], cot_send.at[n])
        wait_bytes(cots.at[same_x], cot_send.at[4 + n])
    wait_bytes(cots.at[same_y], cot_send.at[3])
    for h in range(LOCAL_HEADS):
        wait_bytes(qkv.at[h, :, sent], qkv_send.at[h])
        wait_bytes(atts.at[h, pl.ds(0, 15), c], spread_send.at[h])
        wait_bytes(atts.at[h, :, c], core_send.at[h])

        @pl.when(mine)
        def _():
            wait_bytes(terms.at[h, pl.ds(0, NZ - 1)], term_send.at[h])

        @pl.when(jnp.logical_not(mine))
        def _():
            wait_bytes(terms.at[h], term_send.at[h])

    wait_bytes(qkv.at[:, 0, sent], out_send)


def body(primal, tangent, cotangent):
    prim = jnp.transpose(primal[0], (1, 0, 2))
    tang = jnp.transpose(tangent[0], (1, 0, 2))
    hbm = pl.BlockSpec(memory_space=pl.ANY)
    dma = pltpu.SemaphoreType.DMA
    bf16, f32 = jnp.bfloat16, jnp.float32
    att, tan, wg = pl.pallas_call(
        kernel,
        out_shape=(
            jax.ShapeDtypeStruct((TOKENS, WIDTH), bf16),
            jax.ShapeDtypeStruct((TOKENS, WIDTH), bf16),
            jax.ShapeDtypeStruct((ROWS, 256), f32),
        ),
        in_specs=[hbm] * 3,
        out_specs=(hbm, hbm, pl.BlockSpec(memory_space=pltpu.VMEM)),
        scratch_shapes=[
            pltpu.VMEM((LOCAL_HEADS, 3, SEQ_LEN, 256), bf16),
            pltpu.VMEM((PLANE_TOKENS, QUARTER), bf16),
            pltpu.VMEM((LOCAL_HEADS, SEQ_LEN, HEAD_DIM), bf16),
            pltpu.VMEM((LOCAL_HEADS, SEQ_LEN, HEAD_DIM), bf16),
            pltpu.VMEM((SEQ_LEN, HEAD_DIM), f32),
            pltpu.VMEM((LOCAL_HEADS, PLANE // 2, 2, TOKENS, 256), bf16),
            pltpu.VMEM((QUARTER, 256), f32),
            pltpu.VMEM((LOCAL_HEADS, QUARTER, 256), bf16),
            pltpu.VMEM((LOCAL_HEADS, NZ, ROWS, HEAD_DIM), bf16),
            dma((2,)), dma((2,)), dma((7,)), dma((8,)), dma(()), dma((2, NSEQ)), dma(()),
            dma((2,)), dma((2,)), dma((2,)), dma((2,)), dma((2,)), dma((2,)),
        ],
        compiler_params=pltpu.CompilerParams(
            collective_id=0, has_side_effects=True, vmem_limit_bytes=56 * 2**20
        ),
        cost_estimate=pl.CostEstimate(
            flops=2 * 2 * SEQ_LEN * SEQ_LEN * 128 * 6 + 2 * FEATURES * 256 * SEQ_LEN,
            bytes_accessed=16 * 2**20, transcendentals=2 * SEQ_LEN * SEQ_LEN,
        ),
        name="attention_jvp",
    )(prim, tang, cotangent[0])
    return att[None], tan[None], wg


def solution(mesh):
    return jax.shard_map(
        body,
        mesh=mesh,
        in_specs=(P("dp", "seq", None, None), P("dp", "seq", None, None), P("dp", "seq", None)),
        out_specs=(P("dp", "seq", None), P("dp", "seq", None), P("dp", "seq")),
        check_vma=False,
    )
```
